256 devices in a mesh: dp: 4 (over y_lo, core), ctx: 64 (over y_hi, x, z).
Axes of the slice: x: 4, y: 4 (y_hi: 2, y_lo: 2; y = y_hi * 2 + y_lo), z: 8, core: 2. Of those that a mesh axis runs over, the one named last changes fastest.
Arguments:
- query: bfloat16 [4, 16384, 4096], P('dp', 'ctx'), may hold values from -6 to 6
- key_proj: bfloat16 [4, 16384, 512], P('dp', 'ctx'), may hold values from -6 to 6
- value: bfloat16 [4, 16384, 512], P('dp', 'ctx'), may hold values from -6 to 6
- sinks: float32 [64], replicated, may hold values from 0 to 6
- doc_ids: int32 [4, 16384], P('dp'), may hold values from 0 to 63, never falling along the last dimension, each value on 1 to 512 neighbouring positions
- grad_out: bfloat16 [4, 16384, 4096], P('dp', 'ctx'), may hold values from -6 to 6
Outputs:
- attended: bfloat16 [4, 16384, 4096], P('dp', 'ctx')
- grad_query: bfloat16 [4, 16384, 4096], P('dp', 'ctx')
- grad_key: bfloat16 [4, 16384, 512], P('dp', 'ctx')
- grad_value: bfloat16 [4, 16384, 512], P('dp', 'ctx')
- grad_sinks: float32 [64], replicated
The draws below stay inside these ranges and needn't reach their ends.
Inputs may be any that keep to these rules, and one draw needn't show every extreme that they name: `doc_ids`: each trace's documents are contiguous runs of tokens, numbered upward, each at most 512 tokens long, one exactly so.
All inputs are finite; a program needn't handle non-finite values.
Results may differ from the reference program's by a relative error of at most 0.012.
The reference program's roundings to bfloat16 on the way (of `weights` and `score_grads`) count: a program that leaves them out, or rounds other values in their place, can miss the bound.
Values may be sent and summed in bfloat16 or wider, within the bound.
No kernel may reach another device: no remote copies, remote signals or barrier semaphores. Data moves between devices by JAX's collectives and lax.ppermute only.
A program may use at most 128 MiB of HBM per device.

```python
import math
import jax
import jax.numpy as jnp
import numpy as np
from jax import lax

H = 64
KV = 8
HD = 64
TOK_DEV = 256
SPAN = 2
TRACES = 4
SEQ = 16384
N_CTX = 64


def draw_query(key, part):
    key = jax.random.fold_in(key, 11)
    result = jnp.clip(jax.random.normal(key, (TRACES, SEQ, H * HD), jnp.float32), -4.0, 4.0)
    return result.astype(jnp.bfloat16)


def draw_key_proj(key, part):
    key = jax.random.fold_in(key, 23)
    result = jnp.clip(jax.random.normal(key, (TRACES, SEQ, KV * HD), jnp.float32), -4.0, 4.0)
    return result.astype(jnp.bfloat16)


def shard_levels(key, shape, shards, least, top_value):
    gain = 1.0
    for dim, parts in shards:
        steps = jax.random.uniform(jax.random.fold_in(jax.random.fold_in(key, 6), dim), (parts,), jnp.float32, least / len(shards), top_value / len(shards))
        gain = gain * jnp.repeat(jnp.exp(steps), shape[dim] // parts).reshape((-1,) + (1,) * (len(shape) - 1 - dim))
    return gain


def split_up(count, total, limit, lean):
    weights = [(1 << 20) // math.isqrt(grade ** lean) + 1 for grade in range(2, count + 1)]
    rest, given = total - limit - (count - 1), [1] * (count - 1)
    while rest > 0:
        free = [i for i in range(count - 1) if given[i] < limit]
        mass, remaining = sum([weights[i] for i in free]), rest
        for i in free:
            addition = min(limit - given[i], max(1, remaining * weights[i] // mass), rest)
            given[i] = given[i] + addition
            rest = rest - addition
    return np.array([limit] + given)


def uneven(own_key, number_of, total, reach, lean):
    if number_of == 2:
        one = jax.random.randint(own_key, (), max(1, total - reach), min(reach, total - 1) + 1)
        return jnp.stack([one, total - one])
    tallies = jnp.asarray(split_up(number_of, total, reach, lean), jnp.int32)
    twos = (number_of - 1) // 2
    giver, sink = tallies[1:1 + 2 * twos:2], tallies[2:2 + 2 * twos:2]
    margin = jnp.minimum(giver - 1, reach - sink)
    passed = jax.random.randint(jax.random.fold_in(own_key, 1), (twos,), 0, 1 << 20) % (margin + 1)
    tallies = tallies.at[1:1 + 2 * twos:2].set(giver - passed).at[2:2 + 2 * twos:2].set(sink + passed)
    return tallies[jax.random.permutation(jax.random.fold_in(own_key, 2), number_of)]


def scatter_about(stream_key, dims, scale, reach, shards=(), kind=jnp.bfloat16):
    level = shard_levels(stream_key, dims, shards, -0.22, 0.18) if shards else 1.0
    drawn = jax.random.normal(stream_key, dims, jnp.float32) * scale * level
    return jnp.minimum(jnp.maximum(drawn, -reach), reach).astype(kind)


def setup_inputs(seed: int = 0) -> dict:
    key_of = jax.random.split(jax.random.key(seed), 7)
    return {
        "query": draw_query(jax.random.fold_in(key_of[6], 71), 0),
        "key_proj": draw_key_proj(jax.random.fold_in(key_of[6], 71), 0),
        "value": scatter_about(key_of[2], (TRACES, SEQ, KV * HD), 1.0, 6.0, ((0, 4), (1, 64))),
        "sinks": jnp.clip(jax.random.uniform(key_of[3], (H,), jnp.float32, 0.0, 6.0), 0.0, 6.0),
        "doc_ids": jax.vmap(lambda own: jnp.searchsorted(jnp.cumsum(uneven(own, N_CTX, SEQ, SPAN * TOK_DEV, 2)), jnp.arange(SEQ), side="right"))(jax.random.split(key_of[4], TRACES)).reshape((TRACES, SEQ)).astype(jnp.int32),
        "grad_out": scatter_about(key_of[5], (TRACES, SEQ, H * HD), 1.0, 6.0, ((0, 4), (1, 64))),
    }


score_scale = 0.125


def block_grads(queries, keys_win, values_win, grads, sinks, visible):
    rows = queries.shape[0]
    width = keys_win.shape[0]
    groups = H // KV
    q_heads = queries.reshape(rows, KV, groups, HD).transpose(1, 2, 0, 3).astype(jnp.float32)
    g_heads = grads.reshape(rows, KV, groups, HD).transpose(1, 2, 0, 3).astype(jnp.float32)
    k_heads = keys_win.reshape(width, KV, HD).transpose(1, 0, 2).astype(jnp.float32)
    v_heads = values_win.reshape(width, KV, HD).transpose(1, 0, 2).astype(jnp.float32)
    sink_heads = sinks.reshape(KV, groups)[:, :, None]
    scores = jnp.einsum('kgtd,kld->kgtl', q_heads, k_heads) * score_scale
    scores = jnp.where(visible[None, None], scores, -jnp.inf)
    top = jnp.maximum(jnp.max(scores, axis=-1), sink_heads)
    expo = jnp.exp(scores - top[..., None])
    sink_part = jnp.exp(sink_heads - top)
    denom = jnp.sum(expo, axis=-1) + sink_part
    probs = expo / denom[..., None]
    weights = probs.astype(jnp.bfloat16).astype(jnp.float32)
    attended = jnp.einsum('kgtl,kld->kgtd', weights, v_heads).astype(jnp.bfloat16)
    rowdot = jnp.sum(g_heads * attended.astype(jnp.float32), axis=-1)
    dprobs = jnp.einsum('kgtd,kld->kgtl', g_heads, v_heads)
    score_grads = (probs * (dprobs - rowdot[..., None])).astype(jnp.bfloat16).astype(jnp.float32)
    grad_q = (jnp.einsum('kgtl,kld->kgtd', score_grads, k_heads) * score_scale).astype(jnp.bfloat16)
    grad_k = jnp.einsum('kgtl,kgtd->kld', score_grads, q_heads) * score_scale
    grad_v = jnp.einsum('kgtl,kgtd->kld', weights, g_heads)
    sink_grad = -jnp.sum(sink_part / denom * rowdot, axis=-1).reshape(H)
    attended = attended.transpose(2, 0, 1, 3).reshape(rows, H * HD)
    grad_q = grad_q.transpose(2, 0, 1, 3).reshape(rows, H * HD)
    grad_k = grad_k.transpose(1, 0, 2).reshape(width, KV * HD)
    grad_v = grad_v.transpose(1, 0, 2).reshape(width, KV * HD)
    return attended, grad_q, grad_k, grad_v, sink_grad


def reference(query, key_proj, value, sinks, doc_ids, grad_out):
    block_rows = TOK_DEV
    width = (SPAN + 1) * block_rows
    front = SPAN * block_rows

    def one_trace(items):
        queries, keys_all, values_all, segs, grads = items
        key_pad = jnp.concatenate([jnp.zeros((front, KV * HD), jnp.bfloat16), keys_all], axis=0)
        value_pad = jnp.concatenate([jnp.zeros((front, KV * HD), jnp.bfloat16), values_all], axis=0)
        seg_pad = jnp.concatenate([jnp.full((front,), -1, jnp.int32), segs.astype(jnp.int32)], axis=0)

        def advance(carry, index):
            acc_k, acc_v, acc_sink = carry
            start = (index * block_rows).astype(jnp.int32)
            q_blk = lax.dynamic_slice_in_dim(queries, start, block_rows)
            g_blk = lax.dynamic_slice_in_dim(grads, start, block_rows)
            q_seg = lax.dynamic_slice_in_dim(segs.astype(jnp.int32), start, block_rows)
            k_win = lax.dynamic_slice_in_dim(key_pad, start, width)
            v_win = lax.dynamic_slice_in_dim(value_pad, start, width)
            k_seg = lax.dynamic_slice_in_dim(seg_pad, start, width)
            k_pos = start - front + jnp.arange(width, dtype=jnp.int32)
            q_pos = start + jnp.arange(block_rows, dtype=jnp.int32)
            visible = (q_seg[:, None] == k_seg[None, :]) & (k_pos[None, :] <= q_pos[:, None]) & (k_pos[None, :] >= 0)
            attended, grad_q, grad_k, grad_v, sink_grad = block_grads(q_blk, k_win, v_win, g_blk, sinks, visible)
            acc_k = lax.dynamic_update_slice_in_dim(acc_k, lax.dynamic_slice_in_dim(acc_k, start, width) + grad_k, start, 0)
            acc_v = lax.dynamic_update_slice_in_dim(acc_v, lax.dynamic_slice_in_dim(acc_v, start, width) + grad_v, start, 0)
            return (acc_k, acc_v, acc_sink + sink_grad), (attended, grad_q)

        init = (jnp.zeros((front + SEQ, KV * HD), jnp.float32), jnp.zeros((front + SEQ, KV * HD), jnp.float32), jnp.zeros((H,), jnp.float32))
        (acc_k, acc_v, acc_sink), (outs, grad_qs) = lax.scan(advance, init, jnp.arange(N_CTX, dtype=jnp.int32))
        return (outs.reshape(SEQ, H * HD), grad_qs.reshape(SEQ, H * HD), acc_k[front:].astype(jnp.bfloat16), acc_v[front:].astype(jnp.bfloat16), acc_sink)

    results = lax.map(one_trace, (query, key_proj, value, doc_ids, grad_out))
    return results[0], results[1], results[2], results[3], jnp.sum(results[4], axis=0)
```

```python
import functools

import jax
import jax.numpy as jnp
from jax import lax
from jax.experimental import pallas as pl
from jax.experimental.pallas import tpu as pltpu
from jax.sharding import PartitionSpec as P

H = 64
KV = 8
HD = 64
SPAN = 2
ROWS = 256
TILE = 128
WIN = SPAN * ROWS + TILE
CHUNKS = 2
PAIRS = KV // 2
FAR = 16384.0

score_scale = 0.125


def passed_along(block, axis, distance):
    devices = range(lax.axis_size(axis))
    route = [(i - distance, i) for i in devices if i - distance in devices]
    return lax.ppermute(block, axis, route)


def dot(a, b, dim_a, dim_b):
    return lax.dot_general(
        a, b, (((dim_a,), (dim_b,)), ((), ())), preferred_element_type=jnp.float32
    )


def side_by_side(x):
    return jnp.concatenate([x[:HD], x[HD:]], axis=1)


def stacked(x):
    return jnp.concatenate([x[:, :TILE], x[:, TILE:]], axis=0)


def kernel(first, *refs):
    if not first:
        refs = refs[:8] + refs[10:]
    (q_ref, g_ref, kv2_ref, kv1_ref, kv0_ref, f_ref, t_ref, s_ref) = refs[:8]
    (o_ref, dq_ref, d2_ref, d1_ref, d0_ref, sg_ref) = refs[8:14]
    (kk, vv, kt, vt, pt, dst, qm, gm, acck, accv) = refs[14:]
    lane = lax.broadcasted_iota(jnp.int32, (TILE, 2 * HD), 1)
    even = lane < HD
    key_at = lax.broadcasted_iota(jnp.int32, (TILE, 2 * TILE), 0)
    query_at = lax.broadcasted_iota(jnp.int32, (TILE, 2 * TILE), 1) % TILE
    causal = key_at <= query_at
    for n, ref in enumerate((kv2_ref, kv1_ref, kv0_ref)):
        kt[:, n * ROWS : (n + 1) * ROWS] = ref[:, : 2 * HD].T
        vt[:, n * ROWS : (n + 1) * ROWS] = ref[:, 2 * HD :].T
    kk[:, 2 * HD :] = t_ref[...]
    for h in range(2):
        for n, ref in enumerate((kv2_ref, kv1_ref, kv0_ref)):
            k_head = ref[:, h * HD : (h + 1) * HD]
            v_head = ref[:, (2 + h) * HD : (3 + h) * HD]
            rows = slice(n * ROWS, (n + 1) * ROWS)
            kk[rows, :HD] = k_head
            kk[rows, HD : 2 * HD] = k_head
            vv[rows, :HD] = v_head
            vv[rows, HD:] = v_head
        own = slice(h * HD, (h + 1) * HD)
        for r in range(ROWS // TILE):
            rows = slice(r * TILE, (r + 1) * TILE)
            win = slice(r * TILE, r * TILE + WIN)
            f = f_ref[rows, :]
            for p in range(4):
                lanes = slice(h * 512 + p * 128, h * 512 + (p + 1) * 128)
                cols = slice(p * 2 * TILE, (p + 1) * 2 * TILE)
                line = slice(h * 4 + p, h * 4 + p + 1)
                qp = q_ref[rows, lanes] * jnp.bfloat16(score_scale)
                gp = g_ref[rows, lanes]
                zero = jnp.zeros_like(qp)
                rq = jnp.concatenate([jnp.where(even, qp, zero), jnp.where(even, zero, qp)], 0)
                rg = jnp.concatenate([jnp.where(even, gp, zero), jnp.where(even, zero, gp)], 0)
                rqf = jnp.concatenate([rq, jnp.concatenate([f, f], 0)], 1)
                s = dot(kk[win, :], rqf, 1, 1)
                s = jnp.concatenate(
                    [s[: WIN - TILE], jnp.where(causal, s[WIN - TILE :], -FAR)], 0
                )
                sink = s_ref[line, :]
                top = jnp.maximum(jnp.max(s, axis=0, keepdims=True), sink)
                expo = jnp.exp(s - top)
                sink_part = jnp.exp(sink - top)
                share = 1.0 / (jnp.sum(expo, axis=0, keepdims=True) + sink_part)
                probs = expo * share
                weights = probs.astype(jnp.bfloat16)
                pt[:, cols] = weights
                out = dot(vt[own, win], weights, 1, 0).astype(jnp.bfloat16)
                out = out.astype(jnp.float32)
                g_t = side_by_side(gp.astype(jnp.float32).T)
                rowdot = jnp.sum(g_t * out, axis=0, keepdims=True)
                o_ref[rows, lanes] = stacked(out).T.astype(jnp.bfloat16)
                dp = dot(vv[win, :], rg, 1, 1)
                ds = (probs * (dp - rowdot)).astype(jnp.bfloat16)
                dst[:, cols] = ds
                dq = dot(kt[own, win], ds, 1, 0) * score_scale
                dq_ref[rows, lanes] = stacked(dq).T.astype(jnp.bfloat16)
                sink_grad = -(sink_part * share * rowdot)
                if r == 0:
                    sg_ref[line, :] = sink_grad
                else:
                    sg_ref[line, :] += sink_grad
                qm[cols, :] = rq
                gm[cols, :] = rg
            for acc, big, small in ((acck, dst, qm), (accv, pt, gm)):
                part = dot(big[...], small[...], 1, 0)
                if r == 0:
                    acc[h, :WIN, :] = part
                else:
                    acc[h, TILE:WIN, :] += part[: WIN - TILE]
                    acc[h, WIN:, :] = part[WIN - TILE :]
    lane = lax.broadcasted_iota(jnp.int32, (ROWS, 2 * HD), 1)
    for side, acc in ((0, acck), (1, accv)):
        cols = slice(side * 2 * HD, (side + 1) * 2 * HD)
        for n, ref in enumerate((d2_ref, d1_ref, d0_ref)):
            a = acc[0, n * ROWS : (n + 1) * ROWS, :]
            b = acc[1, n * ROWS : (n + 1) * ROWS, :]
            a = a + pltpu.roll(a, HD, 1)
            b = b + pltpu.roll(b, HD, 1)
            ref[:, cols] = jnp.where(lane < HD, a, b).astype(ref.dtype)


def attend(chunk, queries, grads, kv, f, t, sink_rows, so_far):
    bf, f32 = jnp.bfloat16, jnp.float32
    steps = PAIRS // CHUNKS
    base = chunk * steps
    wide = pl.BlockSpec((ROWS, 1024), lambda i: (0, base + i))
    pair = pl.BlockSpec((ROWS, 256), lambda i: (0, i))
    small = pl.BlockSpec((8, 256), lambda i: (base + i, 0))
    whole = pl.BlockSpec(memory_space=pl.ANY)
    in_specs = [wide, wide, pair, pair, pair]
    in_specs += [pl.BlockSpec((ROWS, 128), lambda i: (0, 0))]
    in_specs += [pl.BlockSpec((3 * ROWS, 128), lambda i: (0, 0)), small]
    args = (queries, grads, *kv, f, t, sink_rows)
    aliases = {}
    if so_far is not None:
        in_specs += [whole, whole]
        args += so_far
        aliases = {8: 0, 9: 1}
    return pl.pallas_call(
        functools.partial(kernel, so_far is None),
        grid=(steps,),
        in_specs=in_specs,
        out_specs=[wide, wide, pair, pair, pair, pl.BlockSpec((8, 256), lambda i: (i, 0))],
        out_shape=[
            jax.ShapeDtypeStruct((ROWS, H * HD), bf),
            jax.ShapeDtypeStruct((ROWS, H * HD), bf),
            jax.ShapeDtypeStruct((ROWS, 256 * steps), bf),
            jax.ShapeDtypeStruct((ROWS, 256 * steps), f32),
            jax.ShapeDtypeStruct((ROWS, 256 * steps), f32),
            jax.ShapeDtypeStruct((8 * steps, 256), f32),
        ],
        scratch_shapes=[
            pltpu.VMEM((3 * ROWS, 256), bf),
            pltpu.VMEM((3 * ROWS, 128), bf),
            pltpu.VMEM((128, 3 * ROWS), bf),
            pltpu.VMEM((128, 3 * ROWS), bf),
            pltpu.VMEM((WIN, 1024), bf),
            pltpu.VMEM((WIN, 1024), bf),
            pltpu.VMEM((1024, 128), bf),
            pltpu.VMEM((1024, 128), bf),
            pltpu.VMEM((2, 3 * ROWS, 128), f32),
            pltpu.VMEM((2, 3 * ROWS, 128), f32),
        ],
        input_output_aliases=aliases,
        compiler_params=pltpu.CompilerParams(vmem_limit_bytes=48 * 1024 * 1024),
    )(*args)


def on_device(query, key_proj, value, sinks, doc_ids, grad_out):
    queries, keys, values, grads = query[0], key_proj[0], value[0], grad_out[0]
    steps = PAIRS // CHUNKS
    own = []
    for c in range(CHUNKS):
        parts = []
        for i in range(c * steps, (c + 1) * steps):
            parts += [keys[:, i * 128 : (i + 1) * 128], values[:, i * 128 : (i + 1) * 128]]
        own.append(jnp.concatenate(parts, axis=1))
    near = [passed_along(x, "ctx", 1) for x in own]
    far = [passed_along(x, "ctx", 1) for x in near]

    start = lax.axis_index("ctx") * ROWS
    front = SPAN * ROWS
    seg_pad = jnp.concatenate([jnp.full((front,), -1, jnp.int32), doc_ids[0]], axis=0)
    k_seg = lax.dynamic_slice_in_dim(seg_pad, start, front + ROWS)
    q_seg = k_seg[front:]
    feature = jnp.arange(128, dtype=jnp.int32)[None, :]
    f = ((feature <= q_seg[:, None]) & (feature < 64)).astype(jnp.bfloat16)
    t = jnp.where((feature > k_seg[:, None]) & (feature < 64), -FAR, 0.0).astype(jnp.bfloat16)
    sink_rows = jnp.repeat(sinks, TILE).reshape(H // 2, 2 * TILE)

    so_far, nearest, sums, sink_sums = None, [], [], []
    for c in range(CHUNKS):
        attended, grad_q, d2, d1, d0, sg = attend(
            c, queries, grads, (far[c], near[c], own[c]), f, t, sink_rows, so_far
        )
        so_far = (attended, grad_q)
        got = passed_along(d2, "ctx", -1).astype(jnp.float32)
        nearest.append((d1 + got).astype(jnp.bfloat16))
        sums.append(d0)
        sink_sums.append(jnp.sum(sg.reshape(-1, TILE), axis=1))
    grad_k, grad_v = [], []
    for c in range(CHUNKS):
        total = sums[c] + passed_along(nearest[c], "ctx", -1).astype(jnp.float32)
        total = total.astype(jnp.bfloat16)
        for i in range(steps):
            grad_k.append(total[:, i * 256 : i * 256 + 128])
            grad_v.append(total[:, i * 256 + 128 : (i + 1) * 256])
    sink_grad = jnp.concatenate(sink_sums)
    devices = lax.axis_size("dp") * lax.axis_size("ctx")
    spread = jnp.broadcast_to(sink_grad[None], (devices, H))
    sink_total = jnp.sum(lax.all_to_all(spread, ("dp", "ctx"), 0, 0, tiled=True), axis=0)
    return (
        attended[None],
        grad_q[None],
        jnp.concatenate(grad_k, axis=1)[None],
        jnp.concatenate(grad_v, axis=1)[None],
        sink_total,
    )


def solution(mesh):
    in_specs = (
        P("dp", "ctx", None),
        P("dp", "ctx", None),
        P("dp", "ctx", None),
        P(),
        P("dp", None),
        P("dp", "ctx", None),
    )
    out_specs = (
        P("dp", "ctx", None),
        P("dp", "ctx", None),
        P("dp", "ctx", None),
        P("dp", "ctx", None),
        P(),
    )
    return jax.shard_map(
        on_device, mesh=mesh, in_specs=in_specs, out_specs=out_specs, check_vma=False
    )
```

```python
import functools

import jax
import jax.numpy as jnp
from jax import lax
from jax.experimental import pallas as pl
from jax.experimental.pallas import tpu as pltpu
from jax.sharding import PartitionSpec as P

H = 64
KV = 8
HD = 64
SPAN = 2
ROWS = 256
TILE = 128
WIN = SPAN * ROWS + TILE
CHUNKS = 2
PAIRS = KV // 2
FAR = 16384.0

score_scale = 0.125


def passed_along(block, axis, distance):
    devices = range(lax.axis_size(axis))
    route = [(i - distance, i) for i in devices if i - distance in devices]
    return lax.ppermute(block, axis, route)


def dot(a, b, dim_a, dim_b):
    return lax.dot_general(
        a, b, (((dim_a,), (dim_b,)), ((), ())), preferred_element_type=jnp.float32
    )


def side_by_side(x):
    return jnp.concatenate([x[:HD], x[HD:]], axis=1)


def stacked(x):
    return jnp.concatenate([x[:, :TILE], x[:, TILE:]], axis=0)


def kernel(first, *refs):
    if not first:
        refs = refs[:8] + refs[10:]
    (q_ref, g_ref, kv2_ref, kv1_ref, kv0_ref, f_ref, t_ref, s_ref) = refs[:8]
    (o_ref, dq_ref, d2_ref, d1_ref, d0_ref, sg_ref) = refs[8:14]
    (kk, vv, kt, vt, pr, pt, dst, qm, gm, acck, accv) = refs[14:]
    lane = lax.broadcasted_iota(jnp.int32, (TILE, 2 * HD), 1)
    even = lane < HD
    key_at = lax.broadcasted_iota(jnp.int32, (TILE, 2 * TILE), 0)
    query_at = lax.broadcasted_iota(jnp.int32, (TILE, 2 * TILE), 1) % TILE
    causal = key_at <= query_at
    for n, ref in enumerate((kv2_ref, kv1_ref, kv0_ref)):
        kt[:, n * ROWS : (n + 1) * ROWS] = ref[:, : 2 * HD].T
        vt[:, n * ROWS : (n + 1) * ROWS] = ref[:, 2 * HD :].T
    for h in range(2):
        kk[h, :, 2 * HD :] = t_ref[...]
        for n, ref in enumerate((kv2_ref, kv1_ref, kv0_ref)):
            k_head = ref[:, h * HD : (h + 1) * HD]
            v_head = ref[:, (2 + h) * HD : (3 + h) * HD]
            rows = slice(n * ROWS, (n + 1) * ROWS)
            kk[h, rows, :HD] = k_head
            kk[h, rows, HD : 2 * HD] = k_head
            vv[h, rows, :HD] = v_head
            vv[h, rows, HD:] = v_head

    def places(n):
        h, r = divmod(n, 2)
        rows = slice(r * TILE, (r + 1) * TILE)
        win = slice(r * TILE, r * TILE + WIN)
        return h, r, rows, win, slice(h * HD, (h + 1) * HD)

    def columns(h, p):
        lanes = slice(h * 512 + p * 128, h * 512 + (p + 1) * 128)
        return lanes, slice(p * 2 * TILE, (p + 1) * 2 * TILE), slice(h * 4 + p, h * 4 + p + 1)

    def apart(x):
        zero = jnp.zeros_like(x)
        return jnp.concatenate([jnp.where(even, x, zero), jnp.where(even, zero, x)], 0)

    kept = {}

    def softmax(n):
        h, r, rows, win, own = places(n)
        f = f_ref[rows, :]
        f = jnp.concatenate([f, f], 0)
        kept[n % 3] = []
        for p in range(4):
            lanes, cols, line = columns(h, p)
            rq = apart(q_ref[rows, lanes] * jnp.bfloat16(score_scale))
            qm[n % 3, cols, :] = rq
            s = dot(kk[h, win, :], jnp.concatenate([rq, f], 1), 1, 1)
            s = jnp.concatenate([s[: WIN - TILE], jnp.where(causal, s[WIN - TILE :], -FAR)], 0)
            sink = s_ref[line, :]
            top = jnp.maximum(jnp.max(s, axis=0, keepdims=True), sink)
            expo = jnp.exp(s - top)
            sink_part = jnp.exp(sink - top)
            share = 1.0 / (jnp.sum(expo, axis=0, keepdims=True) + sink_part)
            probs = expo * share
            pr[n % 3, :, cols] = probs
            pt[n % 3, :, cols] = probs.astype(jnp.bfloat16)
            kept[n % 3].append(sink_part * share)

    def attended(n):
        h, r, rows, win, own = places(n)
        out = dot(vt[own, win], pt[n % 3], 1, 0).astype(jnp.bfloat16)
        kept[n % 3, "out"] = out.astype(jnp.float32)

    def grad_scores(n):
        h, r, rows, win, own = places(n)
        for p in range(4):
            lanes, cols, line = columns(h, p)
            gp = g_ref[rows, lanes]
            rg = apart(gp)
            gm[n % 3, cols, :] = rg
            out = kept[n % 3, "out"][:, cols]
            g_t = side_by_side(gp.astype(jnp.float32).T)
            rowdot = jnp.sum(g_t * out, axis=0, keepdims=True)
            o_ref[rows, lanes] = stacked(out).T.astype(jnp.bfloat16)
            dp = dot(vv[h, win, :], rg, 1, 1)
            dst[n % 3, :, cols] = (pr[n % 3, :, cols] * (dp - rowdot)).astype(jnp.bfloat16)
            sink_grad = -(kept[n % 3][p] * rowdot)
            if r == 0:
                sg_ref[line, :] = sink_grad
            else:
                sg_ref[line, :] += sink_grad

    def grad_query(n):
        h, r, rows, win, own = places(n)
        dq = dot(kt[own, win], dst[n % 3], 1, 0) * score_scale
        for p in range(4):
            lanes, cols, line = columns(h, p)
            dq_ref[rows, lanes] = stacked(dq[:, cols]).T.astype(jnp.bfloat16)

    def gathered(n, acc, big, small):
        h, r, rows, win, own = places(n)
        part = dot(big[n % 3], small[n % 3], 1, 0)
        if r == 0:
            acc[h, :WIN, :] = part
        else:
            acc[h, TILE:WIN, :] += part[: WIN - TILE]
            acc[h, WIN:, :] = part[WIN - TILE :]

    softmax(0)
    for n in range(4):
        if n < 3:
            softmax(n + 1)
        attended(n)
        if n > 0:
            grad_query(n - 1)
            gathered(n - 1, acck, dst, qm)
        grad_scores(n)
        gathered(n, accv, pt, gm)
    grad_query(3)
    gathered(3, acck, dst, qm)

    lane = lax.broadcasted_iota(jnp.int32, (ROWS, 2 * HD), 1)
    for side, acc in ((0, acck), (1, accv)):
        cols = slice(side * 2 * HD, (side + 1) * 2 * HD)
        for n, ref in enumerate((d2_ref, d1_ref, d0_ref)):
            a = acc[0, n * ROWS : (n + 1) * ROWS, :]
            b = acc[1, n * ROWS : (n + 1) * ROWS, :]
            a = a + pltpu.roll(a, HD, 1)
            b = b + pltpu.roll(b, HD, 1)
            ref[:, cols] = jnp.where(lane < HD, a, b).astype(ref.dtype)


def attend(chunk, queries, grads, kv, f, t, sink_rows, so_far):
    bf, f32 = jnp.bfloat16, jnp.float32
    steps = PAIRS // CHUNKS
    base = chunk * steps
    wide = pl.BlockSpec((ROWS, 1024), lambda i: (0, base + i))
    pair = pl.BlockSpec((ROWS, 256), lambda i: (0, i))
    small = pl.BlockSpec((8, 256), lambda i: (base + i, 0))
    whole = pl.BlockSpec(memory_space=pl.ANY)
    in_specs = [wide, wide, pair, pair, pair]
    in_specs += [pl.BlockSpec((ROWS, 128), lambda i: (0, 0))]
    in_specs += [pl.BlockSpec((3 * ROWS, 128), lambda i: (0, 0)), small]
    args = (queries, grads, *kv, f, t, sink_rows)
    aliases = {}
    if so_far is not None:
        in_specs += [whole, whole]
        args += so_far
        aliases = {8: 0, 9: 1}
    return pl.pallas_call(
        functools.partial(kernel, so_far is None),
        grid=(steps,),
        in_specs=in_specs,
        out_specs=[wide, wide, pair, pair, pair, pl.BlockSpec((8, 256), lambda i: (i, 0))],
        out_shape=[
            jax.ShapeDtypeStruct((ROWS, H * HD), bf),
            jax.ShapeDtypeStruct((ROWS, H * HD), bf),
            jax.ShapeDtypeStruct((ROWS, 256 * steps), bf),
            jax.ShapeDtypeStruct((ROWS, 256 * steps), bf),
            jax.ShapeDtypeStruct((ROWS, 256 * steps), f32),
            jax.ShapeDtypeStruct((8 * steps, 256), f32),
        ],
        scratch_shapes=[
            pltpu.VMEM((2, 3 * ROWS, 256), bf),
            pltpu.VMEM((2, 3 * ROWS, 128), bf),
            pltpu.VMEM((128, 3 * ROWS), bf),
            pltpu.VMEM((128, 3 * ROWS), bf),
            pltpu.VMEM((3, WIN, 1024), f32),
            pltpu.VMEM((3, WIN, 1024), bf),
            pltpu.VMEM((3, WIN, 1024), bf),
            pltpu.VMEM((3, 1024, 128), bf),
            pltpu.VMEM((3, 1024, 128), bf),
            pltpu.VMEM((2, 3 * ROWS, 128), f32),
            pltpu.VMEM((2, 3 * ROWS, 128), f32),
        ],
        input_output_aliases=aliases,
        cost_estimate=pl.CostEstimate(
            flops=steps * 16 * 6 * 2 * 256 * WIN * ROWS,
            transcendentals=steps * 16 * WIN * ROWS,
            bytes_accessed=steps * 4 * 1024 * ROWS,
        ),
        compiler_params=pltpu.CompilerParams(vmem_limit_bytes=36 * 1024 * 1024),
    )(*args)


def on_device(query, key_proj, value, sinks, doc_ids, grad_out):
    queries, keys, values, grads = query[0], key_proj[0], value[0], grad_out[0]
    steps = PAIRS // CHUNKS
    own = []
    for c in range(CHUNKS):
        parts = []
        for i in range(c * steps, (c + 1) * steps):
            parts += [keys[:, i * 128 : (i + 1) * 128], values[:, i * 128 : (i + 1) * 128]]
        own.append(jnp.concatenate(parts, axis=1))
    near, far = [], []
    for c, x in enumerate(own):
        if c > 0:
            x, near[c - 1] = lax.optimization_barrier((x, near[c - 1]))
        near.append(passed_along(x, "ctx", 1))
        far.append(passed_along(x, "ctx", 2))

    start = lax.axis_index("ctx") * ROWS
    front = SPAN * ROWS
    seg_pad = jnp.concatenate([jnp.full((front,), -1, jnp.int32), doc_ids[0]], axis=0)
    k_seg = lax.dynamic_slice_in_dim(seg_pad, start, front + ROWS)
    q_seg = k_seg[front:]
    feature = jnp.arange(128, dtype=jnp.int32)[None, :]
    f = ((feature <= q_seg[:, None]) & (feature < 64)).astype(jnp.bfloat16)
    t = jnp.where((feature > k_seg[:, None]) & (feature < 64), -FAR, 0.0).astype(jnp.bfloat16)
    sink_rows = jnp.repeat(sinks, TILE).reshape(H // 2, 2 * TILE)

    so_far, sums, sink_sums = None, [], []
    for c in range(CHUNKS):
        attended, grad_q, d2, d1, d0, sg = attend(
            c, queries, grads, (far[c], near[c], own[c]), f, t, sink_rows, so_far
        )
        so_far = (attended, grad_q)
        sums.append((d0, passed_along(d1, "ctx", -1), passed_along(d2, "ctx", -2)))
        sink_sums.append(jnp.sum(sg.reshape(-1, TILE), axis=1))
    sink_grad = jnp.concatenate(sink_sums)
    sink_grad, sums[:-1] = lax.optimization_barrier((sink_grad, sums[:-1]))
    grad_k, grad_v = [], []
    for d0, from_next, from_second in sums:
        total = d0 + from_next.astype(jnp.float32) + from_second.astype(jnp.float32)
        total = total.astype(jnp.bfloat16)
        for i in range(steps):
            grad_k.append(total[:, i * 256 : i * 256 + 128])
            grad_v.append(total[:, i * 256 + 128 : (i + 1) * 256])
    devices = lax.axis_size("dp") * lax.axis_size("ctx")
    spread = jnp.broadcast_to(sink_grad[None], (devices, H))
    sink_total = jnp.sum(lax.all_to_all(spread, ("dp", "ctx"), 0, 0, tiled=True), axis=0)
    return (
        attended[None],
        grad_q[None],
        jnp.concatenate(grad_k, axis=1)[None],
        jnp.concatenate(grad_v, axis=1)[None],
        sink_total,
    )


def solution(mesh):
    in_specs = (
        P("dp", "ctx", None),
        P("dp", "ctx", None),
        P("dp", "ctx", None),
        P(),
        P("dp", None),
        P("dp", "ctx", None),
    )
    out_specs = (
        P("dp", "ctx", None),
        P("dp", "ctx", None),
        P("dp", "ctx", None),
        P("dp", "ctx", None),
        P(),
    )
    return jax.shard_map(
        on_device, mesh=mesh, in_specs=in_specs, out_specs=out_specs, check_vma=False
    )
```

```python
import functools

import jax
import jax.numpy as jnp
from jax import lax
from jax.experimental import pallas as pl
from jax.experimental.pallas import tpu as pltpu
from jax.sharding import PartitionSpec as P

H = 64
KV = 8
HD = 64
SPAN = 2
ROWS = 256
TILE = 128
WIN = SPAN * ROWS + TILE
CHUNKS = 2
PAIRS = KV // 2
FAR = 16384.0

score_scale = 0.125


def passed_along(block, axis, distance):
    devices = range(lax.axis_size(axis))
    route = [(i - distance, i) for i in devices if i - distance in devices]
    return lax.ppermute(block, axis, route)


def dot(a, b, dim_a, dim_b):
    return lax.dot_general(
        a, b, (((dim_a,), (dim_b,)), ((), ())), preferred_element_type=jnp.float32
    )


def side_by_side(x):
    return jnp.concatenate([x[:HD], x[HD:]], axis=1)


def stacked(x):
    return jnp.concatenate([x[:, :TILE], x[:, TILE:]], axis=0)


def kernel(first, *refs):
    if not first:
        refs = refs[:8] + refs[10:]
    (q_ref, g_ref, kv2_ref, kv1_ref, kv0_ref, f_ref, t_ref, s_ref) = refs[:8]
    (o_ref, dq_ref, d2_ref, d1_ref, d0_ref, sg_ref) = refs[8:14]
    (kk, vv, kt, vt, pr, pt, dst, qm, gm, acck, accv) = refs[14:]
    lane = lax.broadcasted_iota(jnp.int32, (TILE, 2 * HD), 1)
    even = lane < HD
    key_at = lax.broadcasted_iota(jnp.int32, (TILE, 2 * TILE), 0)
    query_at = lax.broadcasted_iota(jnp.int32, (TILE, 2 * TILE), 1) % TILE
    causal = key_at <= query_at
    for n, ref in enumerate((kv2_ref, kv1_ref, kv0_ref)):
        kt[:, n * ROWS : (n + 1) * ROWS] = ref[:, : 2 * HD].T
        vt[:, n * ROWS : (n + 1) * ROWS] = ref[:, 2 * HD :].T
    for h in range(2):
        kk[h, :, 2 * HD :] = t_ref[...]
        for n, ref in enumerate((kv2_ref, kv1_ref, kv0_ref)):
            k_head = ref[:, h * HD : (h + 1) * HD]
            v_head = ref[:, (2 + h) * HD : (3 + h) * HD]
            rows = slice(n * ROWS, (n + 1) * ROWS)
            kk[h, rows, :HD] = k_head
            kk[h, rows, HD : 2 * HD] = k_head
            vv[h, rows, :HD] = v_head
            vv[h, rows, HD:] = v_head

    def places(n):
        h, r = divmod(n, 2)
        rows = slice(r * TILE, (r + 1) * TILE)
        win = slice(r * TILE, r * TILE + WIN)
        return h, r, rows, win, slice(h * HD, (h + 1) * HD)

    def columns(h, p):
        lanes = slice(h * 512 + p * 128, h * 512 + (p + 1) * 128)
        return lanes, slice(p * 2 * TILE, (p + 1) * 2 * TILE), slice(h * 4 + p, h * 4 + p + 1)

    def apart(x):
        zero = jnp.zeros_like(x)
        return jnp.concatenate([jnp.where(even, x, zero), jnp.where(even, zero, x)], 0)

    kept = {}

    def softmax(n):
        h, r, rows, win, own = places(n)
        f = f_ref[rows, :]
        f = jnp.concatenate([f, f], 0)
        kept[n % 3] = []
        for p in range(4):
            lanes, cols, line = columns(h, p)
            rq = apart(q_ref[rows, lanes] * jnp.bfloat16(score_scale))
            qm[n % 3, cols, :] = rq
            s = dot(kk[h, win, :], jnp.concatenate([rq, f], 1), 1, 1)
            s = jnp.concatenate([s[: WIN - TILE], jnp.where(causal, s[WIN - TILE :], -FAR)], 0)
            sink = s_ref[line, :]
            top = jnp.maximum(jnp.max(s, axis=0, keepdims=True), sink)
            expo = jnp.exp(s - top)
            sink_part = jnp.exp(sink - top)
            share = 1.0 / (jnp.sum(expo, axis=0, keepdims=True) + sink_part)
            probs = expo * share
            pr[n % 3, :, cols] = probs
            pt[n % 3, :, cols] = probs.astype(jnp.bfloat16)
            kept[n % 3].append(sink_part * share)

    def attended(n):
        h, r, rows, win, own = places(n)
        out = dot(vt[own, win], pt[n % 3], 1, 0).astype(jnp.bfloat16)
        kept[n % 3, "out"] = out.astype(jnp.float32)

    def grad_scores(n):
        h, r, rows, win, own = places(n)
        for p in range(4):
            lanes, cols, line = columns(h, p)
            gp = g_ref[rows, lanes]
            rg = apart(gp)
            gm[n % 3, cols, :] = rg
            out = kept[n % 3, "out"][:, cols]
            g_t = side_by_side(gp.astype(jnp.float32).T)
            rowdot = jnp.sum(g_t * out, axis=0, keepdims=True)
            o_ref[rows, lanes] = stacked(out).T.astype(jnp.bfloat16)
            dp = dot(vv[h, win, :], rg, 1, 1)
            dst[n % 3, :, cols] = (pr[n % 3, :, cols] * (dp - rowdot)).astype(jnp.bfloat16)
            sink_grad = -(kept[n % 3][p] * rowdot)
            if r == 0:
                sg_ref[line, :] = sink_grad
            else:
                sg_ref[line, :] += sink_grad

    def grad_query(n):
        h, r, rows, win, own = places(n)
        dq = dot(kt[own, win], dst[n % 3], 1, 0) * score_scale
        for p in range(4):
            lanes, cols, line = columns(h, p)
            dq_ref[rows, lanes] = stacked(dq[:, cols]).T.astype(jnp.bfloat16)

    def gathered(n, acc, big, small):
        h, r, rows, win, own = places(n)
        part = dot(big[n % 3], small[n % 3], 1, 0)
        if r == 0:
            acc[h, :WIN, :] = part
        else:
            acc[h, TILE:WIN, :] += part[: WIN - TILE]
            acc[h, WIN:, :] = part[WIN - TILE :]

    softmax(0)
    for n in range(4):
        if n < 3:
            softmax(n + 1)
        attended(n)
        if n > 0:
            grad_query(n - 1)
            gathered(n - 1, acck, dst, qm)
        grad_scores(n)
        gathered(n, accv, pt, gm)
    grad_query(3)
    gathered(3, acck, dst, qm)

    lane = lax.broadcasted_iota(jnp.int32, (ROWS, 2 * HD), 1)
    for side, acc in ((0, acck), (1, accv)):
        cols = slice(side * 2 * HD, (side + 1) * 2 * HD)
        for n, ref in enumerate((d2_ref, d1_ref, d0_ref)):
            a = acc[0, n * ROWS : (n + 1) * ROWS, :]
            b = acc[1, n * ROWS : (n + 1) * ROWS, :]
            a = a + pltpu.roll(a, HD, 1)
            b = b + pltpu.roll(b, HD, 1)
            ref[:, cols] = jnp.where(lane < HD, a, b).astype(ref.dtype)


def attend(chunk, queries, grads, kv, f, t, sink_rows, so_far):
    bf, f32 = jnp.bfloat16, jnp.float32
    steps = PAIRS // CHUNKS
    base = chunk * steps
    wide = pl.BlockSpec((ROWS, 1024), lambda i: (0, base + i))
    pair = pl.BlockSpec((ROWS, 256), lambda i: (0, i))
    small = pl.BlockSpec((8, 256), lambda i: (base + i, 0))
    whole = pl.BlockSpec(memory_space=pl.ANY)
    in_specs = [wide, wide, pair, pair, pair]
    in_specs += [pl.BlockSpec((ROWS, 128), lambda i: (0, 0))]
    in_specs += [pl.BlockSpec((3 * ROWS, 128), lambda i: (0, 0)), small]
    queries = pltpu.with_memory_space_constraint(queries, pltpu.HBM)
    grads = pltpu.with_memory_space_constraint(grads, pltpu.HBM)
    args = (queries, grads, *kv, f, t, sink_rows)
    aliases = {}
    if so_far is not None:
        in_specs += [whole, whole]
        args += so_far
        aliases = {8: 0, 9: 1}
    return pl.pallas_call(
        functools.partial(kernel, so_far is None),
        grid=(steps,),
        in_specs=in_specs,
        out_specs=[wide, wide, pair, pair, pair, pl.BlockSpec((8, 256), lambda i: (i, 0))],
        out_shape=[
            pltpu.HBM((ROWS, H * HD), bf),
            pltpu.HBM((ROWS, H * HD), bf),
            jax.ShapeDtypeStruct((ROWS, 256 * steps), bf),
            jax.ShapeDtypeStruct((ROWS, 256 * steps), bf),
            jax.ShapeDtypeStruct((ROWS, 256 * steps), f32),
            jax.ShapeDtypeStruct((8 * steps, 256), f32),
        ],
        scratch_shapes=[
            pltpu.VMEM((2, 3 * ROWS, 256), bf),
            pltpu.VMEM((2, 3 * ROWS, 128), bf),
            pltpu.VMEM((128, 3 * ROWS), bf),
            pltpu.VMEM((128, 3 * ROWS), bf),
            pltpu.VMEM((3, WIN, 1024), f32),
            pltpu.VMEM((3, WIN, 1024), bf),
            pltpu.VMEM((3, WIN, 1024), bf),
            pltpu.VMEM((3, 1024, 128), bf),
            pltpu.VMEM((3, 1024, 128), bf),
            pltpu.VMEM((2, 3 * ROWS, 128), f32),
            pltpu.VMEM((2, 3 * ROWS, 128), f32),
        ],
        input_output_aliases=aliases,
        cost_estimate=pl.CostEstimate(
            flops=steps * 16 * 6 * 2 * 256 * WIN * ROWS,
            transcendentals=steps * 16 * WIN * ROWS,
            bytes_accessed=steps * 4 * 1024 * ROWS,
        ),
        compiler_params=pltpu.CompilerParams(vmem_limit_bytes=36 * 1024 * 1024),
    )(*args)


def on_device(query, key_proj, value, sinks, doc_ids, grad_out):
    queries, keys, values, grads = query[0], key_proj[0], value[0], grad_out[0]
    steps = PAIRS // CHUNKS
    own = []
    for c in range(CHUNKS):
        parts = []
        for i in range(c * steps, (c + 1) * steps):
            parts += [keys[:, i * 128 : (i + 1) * 128], values[:, i * 128 : (i + 1) * 128]]
        own.append(jnp.concatenate(parts, axis=1))
    near = [passed_along(x, "ctx", 1) for x in own]
    far = []
    for c, x in enumerate(near):
        if c > 0:
            x, far[c - 1] = lax.optimization_barrier((x, far[c - 1]))
        far.append(passed_along(x, "ctx", 1))

    start = lax.axis_index("ctx") * ROWS
    front = SPAN * ROWS
    seg_pad = jnp.concatenate([jnp.full((front,), -1, jnp.int32), doc_ids[0]], axis=0)
    k_seg = lax.dynamic_slice_in_dim(seg_pad, start, front + ROWS)
    q_seg = k_seg[front:]
    feature = jnp.arange(128, dtype=jnp.int32)[None, :]
    f = ((feature <= q_seg[:, None]) & (feature < 64)).astype(jnp.bfloat16)
    t = jnp.where((feature > k_seg[:, None]) & (feature < 64), -FAR, 0.0).astype(jnp.bfloat16)
    sink_rows = jnp.repeat(sinks, TILE).reshape(H // 2, 2 * TILE)

    so_far, sums, sink_sums = None, [], []
    for c in range(CHUNKS):
        attended, grad_q, d2, d1, d0, sg = attend(
            c, queries, grads, (far[c], near[c], own[c]), f, t, sink_rows, so_far
        )
        so_far = (attended, grad_q)
        sums.append((d0, passed_along(d1, "ctx", -1), passed_along(d2, "ctx", -2)))
        sink_sums.append(jnp.sum(sg.reshape(-1, TILE), axis=1))
    sink_grad = jnp.concatenate(sink_sums)
    sink_grad, sums[:-1] = lax.optimization_barrier((sink_grad, sums[:-1]))
    grad_k, grad_v = [], []
    for d0, from_next, from_second in sums:
        total = d0 + from_next.astype(jnp.float32) + from_second.astype(jnp.float32)
        total = total.astype(jnp.bfloat16)
        for i in range(steps):
            grad_k.append(total[:, i * 256 : i * 256 + 128])
            grad_v.append(total[:, i * 256 + 128 : (i + 1) * 256])
    devices = lax.axis_size("dp") * lax.axis_size("ctx")
    spread = jnp.broadcast_to(sink_grad[None], (devices, H))
    sink_total = jnp.sum(lax.all_to_all(spread, ("dp", "ctx"), 0, 0, tiled=True), axis=0)
    return (
        attended[None],
        grad_q[None],
        jnp.concatenate(grad_k, axis=1)[None],
        jnp.concatenate(grad_v, axis=1)[None],
        sink_total,
    )


def solution(mesh):
    in_specs = (
        P("dp", "ctx", None),
        P("dp", "ctx", None),
        P("dp", "ctx", None),
        P(),
        P("dp", None),
        P("dp", "ctx", None),
    )
    out_specs = (
        P("dp", "ctx", None),
        P("dp", "ctx", None),
        P("dp", "ctx", None),
        P("dp", "ctx", None),
        P(),
    )
    return jax.shard_map(
        on_device, mesh=mesh, in_specs=in_specs, out_specs=out_specs, check_vma=False
    )
```

```python
import functools

import jax
import jax.numpy as jnp
from jax import lax
from jax.experimental import pallas as pl
from jax.experimental.pallas import tpu as pltpu
from jax.sharding import PartitionSpec as P

H = 64
KV = 8
HD = 64
SPAN = 2
ROWS = 256
TILE = 128
WIN = SPAN * ROWS + TILE
CHUNKS = 2
PAIRS = KV // 2
FAR = 16384.0

score_scale = 0.125


def passed_along(block, axis, distance):
    devices = range(lax.axis_size(axis))
    route = [(i - distance, i) for i in devices if i - distance in devices]
    return lax.ppermute(block, axis, route)


def dot(a, b, dim_a, dim_b):
    return lax.dot_general(
        a, b, (((dim_a,), (dim_b,)), ((), ())), preferred_element_type=jnp.float32
    )


def side_by_side(x):
    return jnp.concatenate([x[:HD], x[HD:]], axis=1)


def stacked(x):
    return jnp.concatenate([x[:, :TILE], x[:, TILE:]], axis=0)


def kernel(first, *refs):
    if not first:
        refs = refs[:8] + refs[10:]
    (q_ref, g_ref, kv2_ref, kv1_ref, kv0_ref, f_ref, t_ref, s_ref) = refs[:8]
    (o_ref, dq_ref, d2_ref, d1_ref, d0_ref, sg_ref) = refs[8:14]
    (kk, vv, kt, vt, pr, pt, dst, qm, gm, acck, accv) = refs[14:]
    lane = lax.broadcasted_iota(jnp.int32, (TILE, 2 * HD), 1)
    even = lane < HD
    key_at = lax.broadcasted_iota(jnp.int32, (TILE, 2 * TILE), 0)
    query_at = lax.broadcasted_iota(jnp.int32, (TILE, 2 * TILE), 1) % TILE
    causal = key_at <= query_at
    for n, ref in enumerate((kv2_ref, kv1_ref, kv0_ref)):
        kt[:, n * ROWS : (n + 1) * ROWS] = ref[:, : 2 * HD].T
        vt[:, n * ROWS : (n + 1) * ROWS] = ref[:, 2 * HD :].T
    for h in range(2):
        kk[h, :, 2 * HD :] = t_ref[...]
        for n, ref in enumerate((kv2_ref, kv1_ref, kv0_ref)):
            k_head = ref[:, h * HD : (h + 1) * HD]
            v_head = ref[:, (2 + h) * HD : (3 + h) * HD]
            rows = slice(n * ROWS, (n + 1) * ROWS)
            kk[h, rows, :HD] = k_head
            kk[h, rows, HD : 2 * HD] = k_head
            vv[h, rows, :HD] = v_head
            vv[h, rows, HD:] = v_head

    def places(n):
        h, r = divmod(n, 2)
        rows = slice(r * TILE, (r + 1) * TILE)
        win = slice(r * TILE, r * TILE + WIN)
        return h, r, rows, win, slice(h * HD, (h + 1) * HD)

    def columns(h, p):
        lanes = slice(h * 512 + p * 128, h * 512 + (p + 1) * 128)
        return lanes, slice(p * 2 * TILE, (p + 1) * 2 * TILE), slice(h * 4 + p, h * 4 + p + 1)

    def apart(x):
        zero = jnp.zeros_like(x)
        return jnp.concatenate([jnp.where(even, x, zero), jnp.where(even, zero, x)], 0)

    kept = {}

    def softmax(n):
        h, r, rows, win, own = places(n)
        f = f_ref[rows, :]
        f = jnp.concatenate([f, f], 0)
        kept[n % 3] = []
        for p in range(4):
            lanes, cols, line = columns(h, p)
            rq = apart(q_ref[rows, lanes] * jnp.bfloat16(score_scale))
            qm[n % 3, cols, :] = rq
            s = dot(kk[h, win, :], jnp.concatenate([rq, f], 1), 1, 1)
            s = jnp.concatenate([s[: WIN - TILE], jnp.where(causal, s[WIN - TILE :], -FAR)], 0)
            sink = s_ref[line, :]
            top = jnp.maximum(jnp.max(s, axis=0, keepdims=True), sink)
            expo = jnp.exp(s - top)
            sink_part = jnp.exp(sink - top)
            share = 1.0 / (jnp.sum(expo, axis=0, keepdims=True) + sink_part)
            probs = expo * share
            pr[n % 3, :, cols] = probs
            pt[n % 3, :, cols] = probs.astype(jnp.bfloat16)
            kept[n % 3].append(sink_part * share)

    def attended(n):
        h, r, rows, win, own = places(n)
        out = dot(vt[own, win], pt[n % 3], 1, 0).astype(jnp.bfloat16)
        kept[n % 3, "out"] = out.astype(jnp.float32)

    def grad_scores(n):
        h, r, rows, win, own = places(n)
        for p in range(4):
            lanes, cols, line = columns(h, p)
            gp = g_ref[rows, lanes]
            rg = apart(gp)
            gm[n % 3, cols, :] = rg
            out = kept[n % 3, "out"][:, cols]
            g_t = side_by_side(gp.astype(jnp.float32).T)
            rowdot = jnp.sum(g_t * out, axis=0, keepdims=True)
            o_ref[rows, lanes] = stacked(out).T.astype(jnp.bfloat16)
            dp = dot(vv[h, win, :], rg, 1, 1)
            dst[n % 3, :, cols] = (pr[n % 3, :, cols] * (dp - rowdot)).astype(jnp.bfloat16)
            sink_grad = -(kept[n % 3][p] * rowdot)
            if r == 0:
                sg_ref[line, :] = sink_grad
            else:
                sg_ref[line, :] += sink_grad

    def grad_query(n):
        h, r, rows, win, own = places(n)
        dq = dot(kt[own, win], dst[n % 3], 1, 0) * score_scale
        for p in range(4):
            lanes, cols, line = columns(h, p)
            dq_ref[rows, lanes] = stacked(dq[:, cols]).T.astype(jnp.bfloat16)

    def gathered(n, acc, big, small):
        h, r, rows, win, own = places(n)
        part = dot(big[n % 3], small[n % 3], 1, 0)
        if r == 0:
            acc[h, :WIN, :] = part
        else:
            acc[h, TILE:WIN, :] += part[: WIN - TILE]
            acc[h, WIN:, :] = part[WIN - TILE :]

    softmax(0)
    for n in range(4):
        if n < 3:
            softmax(n + 1)
        attended(n)
        if n > 0:
            grad_query(n - 1)
            gathered(n - 1, acck, dst, qm)
        grad_scores(n)
        gathered(n, accv, pt, gm)
    grad_query(3)
    gathered(3, acck, dst, qm)

    lane = lax.broadcasted_iota(jnp.int32, (ROWS, 2 * HD), 1)
    for side, acc in ((0, acck), (1, accv)):
        cols = slice(side * 2 * HD, (side + 1) * 2 * HD)
        for n, ref in enumerate((d2_ref, d1_ref, d0_ref)):
            a = acc[0, n * ROWS : (n + 1) * ROWS, :]
            b = acc[1, n * ROWS : (n + 1) * ROWS, :]
            a = a + pltpu.roll(a, HD, 1)
            b = b + pltpu.roll(b, HD, 1)
            ref[:, cols] = jnp.where(lane < HD, a, b).astype(ref.dtype)


def attend(chunk, queries, grads, kv, f, t, sink_rows, so_far):
    bf, f32 = jnp.bfloat16, jnp.float32
    steps = PAIRS // CHUNKS
    base = chunk * steps
    wide = pl.BlockSpec((ROWS, 1024), lambda i: (0, base + i))
    pair = pl.BlockSpec((ROWS, 256), lambda i: (0, i))
    small = pl.BlockSpec((8, 256), lambda i: (base + i, 0))
    whole = pl.BlockSpec(memory_space=pl.ANY)
    in_specs = [wide, wide, pair, pair, pair]
    in_specs += [pl.BlockSpec((ROWS, 128), lambda i: (0, 0))]
    in_specs += [pl.BlockSpec((3 * ROWS, 128), lambda i: (0, 0)), small]
    queries = pltpu.with_memory_space_constraint(queries, pltpu.HBM)
    grads = pltpu.with_memory_space_constraint(grads, pltpu.HBM)
    args = (queries, grads, *kv, f, t, sink_rows)
    aliases = {}
    if so_far is not None:
        in_specs += [whole, whole]
        args += so_far
        aliases = {8: 0, 9: 1}
    return pl.pallas_call(
        functools.partial(kernel, so_far is None),
        grid=(steps,),
        in_specs=in_specs,
        out_specs=[wide, wide, pair, pair, pair, pl.BlockSpec((8, 256), lambda i: (i, 0))],
        out_shape=[
            pltpu.HBM((ROWS, H * HD), bf),
            pltpu.HBM((ROWS, H * HD), bf),
            jax.ShapeDtypeStruct((ROWS, 256 * steps), bf),
            jax.ShapeDtypeStruct((ROWS, 256 * steps), f32),
            jax.ShapeDtypeStruct((ROWS, 256 * steps), f32),
            jax.ShapeDtypeStruct((8 * steps, 256), f32),
        ],
        scratch_shapes=[
            pltpu.VMEM((2, 3 * ROWS, 256), bf),
            pltpu.VMEM((2, 3 * ROWS, 128), bf),
            pltpu.VMEM((128, 3 * ROWS), bf),
            pltpu.VMEM((128, 3 * ROWS), bf),
            pltpu.VMEM((3, WIN, 1024), f32),
            pltpu.VMEM((3, WIN, 1024), bf),
            pltpu.VMEM((3, WIN, 1024), bf),
            pltpu.VMEM((3, 1024, 128), bf),
            pltpu.VMEM((3, 1024, 128), bf),
            pltpu.VMEM((2, 3 * ROWS, 128), f32),
            pltpu.VMEM((2, 3 * ROWS, 128), f32),
        ],
        input_output_aliases=aliases,
        cost_estimate=pl.CostEstimate(
            flops=steps * 16 * 6 * 2 * 256 * WIN * ROWS,
            transcendentals=steps * 16 * WIN * ROWS,
            bytes_accessed=steps * 4 * 1024 * ROWS,
        ),
        compiler_params=pltpu.CompilerParams(vmem_limit_bytes=36 * 1024 * 1024),
    )(*args)


def on_device(query, key_proj, value, sinks, doc_ids, grad_out):
    queries, keys, values, grads = query[0], key_proj[0], value[0], grad_out[0]
    steps = PAIRS // CHUNKS
    own = []
    for c in range(CHUNKS):
        parts = []
        for i in range(c * steps, (c + 1) * steps):
            parts += [keys[:, i * 128 : (i + 1) * 128], values[:, i * 128 : (i + 1) * 128]]
        own.append(jnp.concatenate(parts, axis=1))
    near = [passed_along(x, "ctx", 1) for x in own]
    far = []
    for c, x in enumerate(near):
        if c > 0:
            x, far[c - 1] = lax.optimization_barrier((x, far[c - 1]))
        far.append(passed_along(x, "ctx", 1))

    start = lax.axis_index("ctx") * ROWS
    front = SPAN * ROWS
    seg_pad = jnp.concatenate([jnp.full((front,), -1, jnp.int32), doc_ids[0]], axis=0)
    k_seg = lax.dynamic_slice_in_dim(seg_pad, start, front + ROWS)
    q_seg = k_seg[front:]
    feature = jnp.arange(128, dtype=jnp.int32)[None, :]
    f = ((feature <= q_seg[:, None]) & (feature < 64)).astype(jnp.bfloat16)
    t = jnp.where((feature > k_seg[:, None]) & (feature < 64), -FAR, 0.0).astype(jnp.bfloat16)
    sink_rows = jnp.repeat(sinks, TILE).reshape(H // 2, 2 * TILE)

    so_far, parts = None, []
    for c in range(CHUNKS):
        attended, grad_q, *rest = attend(
            c, queries, grads, (far[c], near[c], own[c]), f, t, sink_rows, so_far
        )
        so_far = (attended, grad_q)
        parts.append(rest)
        if c == 0:
            got = passed_along(rest[0], "ctx", -1)
    (_, near_0, own_0, sinks_0), (far_1, near_1, own_1, sinks_1) = parts

    def joined(share, came):
        return (share + came.astype(jnp.float32)).astype(jnp.bfloat16)

    half = 256 * steps
    got, far_1 = lax.optimization_barrier((got, far_1))
    both = jnp.concatenate([far_1, joined(near_0, got)], axis=1)
    both = passed_along(both, "ctx", -1)
    sink_grad = jnp.concatenate([jnp.sum(x.reshape(-1, TILE), axis=1) for x in (sinks_0, sinks_1)])
    devices = lax.axis_size("dp") * lax.axis_size("ctx")
    spread = jnp.broadcast_to(sink_grad[None], (devices, H))
    spread = lax.all_to_all(spread, ("dp", "ctx"), 0, 0, tiled=True)
    both, spread = lax.optimization_barrier((both, spread))
    last = passed_along(joined(near_1, both[:, :half]), "ctx", -1)
    sink_total = jnp.sum(spread, axis=0)
    grad_k, grad_v = [], []
    for total in (joined(own_0, both[:, half:]), joined(own_1, last)):
        for i in range(steps):
            grad_k.append(total[:, i * 256 : i * 256 + 128])
            grad_v.append(total[:, i * 256 + 128 : (i + 1) * 256])
    return (
        attended[None],
        grad_q[None],
        jnp.concatenate(grad_k, axis=1)[None],
        jnp.concatenate(grad_v, axis=1)[None],
        sink_total,
    )


def solution(mesh):
    in_specs = (
        P("dp", "ctx", None),
        P("dp", "ctx", None),
        P("dp", "ctx", None),
        P(),
        P("dp", None),
        P("dp", "ctx", None),
    )
    out_specs = (
        P("dp", "ctx", None),
        P("dp", "ctx", None),
        P("dp", "ctx", None),
        P("dp", "ctx", None),
        P(),
    )
    return jax.shard_map(
        on_device, mesh=mesh, in_specs=in_specs, out_specs=out_specs, check_vma=False
    )
```

```python
import functools

import jax
import jax.numpy as jnp
from jax import lax
from jax.experimental import pallas as pl
from jax.experimental.pallas import tpu as pltpu
from jax.sharding import PartitionSpec as P

H = 64
KV = 8
HD = 64
SPAN = 2
ROWS = 256
TILE = 128
WIN = SPAN * ROWS + TILE
CHUNKS = 2
PAIRS = KV // 2
FAR = 16384.0

score_scale = 0.125


def passed_along(block, axis, distance):
    devices = range(lax.axis_size(axis))
    route = [(i - distance, i) for i in devices if i - distance in devices]
    return lax.ppermute(block, axis, route)


def dot(a, b, dim_a, dim_b):
    return lax.dot_general(
        a, b, (((dim_a,), (dim_b,)), ((), ())), preferred_element_type=jnp.float32
    )


def side_by_side(x):
    return jnp.concatenate([x[:HD], x[HD:]], axis=1)


def stacked(x):
    return jnp.concatenate([x[:, :TILE], x[:, TILE:]], axis=0)


def kernel(first, *refs):
    if not first:
        refs = refs[:8] + refs[10:]
    (q_ref, g_ref, kv2_ref, kv1_ref, kv0_ref, f_ref, t_ref, s_ref) = refs[:8]
    (o_ref, dq_ref, d2_ref, d1_ref, d0_ref, sg_ref) = refs[8:14]
    (kk, vv, kt, vt, pr, pt, dst, qm, gm, acck, accv) = refs[14:]
    lane = lax.broadcasted_iota(jnp.int32, (TILE, 2 * HD), 1)
    even = lane < HD
    key_at = lax.broadcasted_iota(jnp.int32, (TILE, 2 * TILE), 0)
    query_at = lax.broadcasted_iota(jnp.int32, (TILE, 2 * TILE), 1) % TILE
    causal = key_at <= query_at
    for n, ref in enumerate((kv2_ref, kv1_ref, kv0_ref)):
        kt[:, n * ROWS : (n + 1) * ROWS] = ref[:, : 2 * HD].T
        vt[:, n * ROWS : (n + 1) * ROWS] = ref[:, 2 * HD :].T
    for h in range(2):
        kk[h, :, 2 * HD :] = t_ref[...]
        for n, ref in enumerate((kv2_ref, kv1_ref, kv0_ref)):
            k_head = ref[:, h * HD : (h + 1) * HD]
            v_head = ref[:, (2 + h) * HD : (3 + h) * HD]
            rows = slice(n * ROWS, (n + 1) * ROWS)
            kk[h, rows, :HD] = k_head
            kk[h, rows, HD : 2 * HD] = k_head
            vv[h, rows, :HD] = v_head
            vv[h, rows, HD:] = v_head

    def places(n):
        h, r = divmod(n, 2)
        rows = slice(r * TILE, (r + 1) * TILE)
        win = slice(r * TILE, r * TILE + WIN)
        return h, r, rows, win, slice(h * HD, (h + 1) * HD)

    def columns(h, p):
        lanes = slice(h * 512 + p * 128, h * 512 + (p + 1) * 128)
        return lanes, slice(p * 2 * TILE, (p + 1) * 2 * TILE), slice(h * 4 + p, h * 4 + p + 1)

    def apart(x):
        zero = jnp.zeros_like(x)
        return jnp.concatenate([jnp.where(even, x, zero), jnp.where(even, zero, x)], 0)

    kept = {}

    def softmax(n):
        h, r, rows, win, own = places(n)
        f = f_ref[rows, :]
        f = jnp.concatenate([f, f], 0)
        kept[n % 3] = []
        for p in range(4):
            lanes, cols, line = columns(h, p)
            rq = apart(q_ref[rows, lanes] * jnp.bfloat16(score_scale))
            qm[n % 3, cols, :] = rq
            s = dot(kk[h, win, :], jnp.concatenate([rq, f], 1), 1, 1)
            s = jnp.concatenate([s[: WIN - TILE], jnp.where(causal, s[WIN - TILE :], -FAR)], 0)
            sink = s_ref[line, :]
            top = jnp.maximum(jnp.max(s, axis=0, keepdims=True), sink)
            expo = jnp.exp(s - top)
            sink_part = jnp.exp(sink - top)
            share = 1.0 / (jnp.sum(expo, axis=0, keepdims=True) + sink_part)
            probs = expo * share
            pr[n % 3, :, cols] = probs
            pt[n % 3, :, cols] = probs.astype(jnp.bfloat16)
            kept[n % 3].append(sink_part * share)

    def attended(n):
        h, r, rows, win, own = places(n)
        out = dot(vt[own, win], pt[n % 3], 1, 0).astype(jnp.bfloat16)
        kept[n % 3, "out"] = out.astype(jnp.float32)

    def grad_scores(n):
        h, r, rows, win, own = places(n)
        for p in range(4):
            lanes, cols, line = columns(h, p)
            gp = g_ref[rows, lanes]
            rg = apart(gp)
            gm[n % 3, cols, :] = rg
            out = kept[n % 3, "out"][:, cols]
            g_t = side_by_side(gp.astype(jnp.float32).T)
            rowdot = jnp.sum(g_t * out, axis=0, keepdims=True)
            o_ref[rows, lanes] = stacked(out).T.astype(jnp.bfloat16)
            dp = dot(vv[h, win, :], rg, 1, 1)
            dst[n % 3, :, cols] = (pr[n % 3, :, cols] * (dp - rowdot)).astype(jnp.bfloat16)
            sink_grad = -(kept[n % 3][p] * rowdot)
            if r == 0:
                sg_ref[line, :] = sink_grad
            else:
                sg_ref[line, :] += sink_grad

    def grad_query(n):
        h, r, rows, win, own = places(n)
        dq = dot(kt[own, win], dst[n % 3], 1, 0) * score_scale
        for p in range(4):
            lanes, cols, line = columns(h, p)
            dq_ref[rows, lanes] = stacked(dq[:, cols]).T.astype(jnp.bfloat16)

    def gathered(n, acc, big, small):
        h, r, rows, win, own = places(n)
        part = dot(big[n % 3], small[n % 3], 1, 0)
        if r == 0:
            acc[h, :WIN, :] = part
        else:
            acc[h, TILE:WIN, :] += part[: WIN - TILE]
            acc[h, WIN:, :] = part[WIN - TILE :]

    softmax(0)
    for n in range(4):
        if n < 3:
            softmax(n + 1)
        attended(n)
        if n > 0:
            grad_query(n - 1)
            gathered(n - 1, acck, dst, qm)
        grad_scores(n)
        gathered(n, accv, pt, gm)
    grad_query(3)
    gathered(3, acck, dst, qm)

    lane = lax.broadcasted_iota(jnp.int32, (ROWS, 2 * HD), 1)
    for side, acc in ((0, acck), (1, accv)):
        cols = slice(side * 2 * HD, (side + 1) * 2 * HD)
        for n, ref in enumerate((d2_ref, d1_ref, d0_ref)):
            a = acc[0, n * ROWS : (n + 1) * ROWS, :]
            b = acc[1, n * ROWS : (n + 1) * ROWS, :]
            a = a + pltpu.roll(a, HD, 1)
            b = b + pltpu.roll(b, HD, 1)
            ref[:, cols] = jnp.where(lane < HD, a, b).astype(ref.dtype)


def attend(chunk, queries, grads, kv, f, t, sink_rows, so_far):
    bf, f32 = jnp.bfloat16, jnp.float32
    steps = PAIRS // CHUNKS
    base = chunk * steps
    wide = pl.BlockSpec((ROWS, 1024), lambda i: (0, base + i))
    pair = pl.BlockSpec((ROWS, 256), lambda i: (0, i))
    small = pl.BlockSpec((8, 256), lambda i: (base + i, 0))
    whole = pl.BlockSpec(memory_space=pl.ANY)
    in_specs = [wide, wide, pair, pair, pair]
    in_specs += [pl.BlockSpec((ROWS, 128), lambda i: (0, 0))]
    in_specs += [pl.BlockSpec((3 * ROWS, 128), lambda i: (0, 0)), small]
    queries = pltpu.with_memory_space_constraint(queries, pltpu.HBM)
    grads = pltpu.with_memory_space_constraint(grads, pltpu.HBM)
    args = (queries, grads, *kv, f, t, sink_rows)
    aliases = {}
    if so_far is not None:
        in_specs += [whole, whole]
        args += so_far
        aliases = {8: 0, 9: 1}
    return pl.pallas_call(
        functools.partial(kernel, so_far is None),
        grid=(steps,),
        in_specs=in_specs,
        out_specs=[wide, wide, pair, pair, pair, pl.BlockSpec((8, 256), lambda i: (i, 0))],
        out_shape=[
            pltpu.HBM((ROWS, H * HD), bf),
            pltpu.HBM((ROWS, H * HD), bf),
            jax.ShapeDtypeStruct((ROWS, 256 * steps), bf),
            jax.ShapeDtypeStruct((ROWS, 256 * steps), f32),
            jax.ShapeDtypeStruct((ROWS, 256 * steps), f32),
            jax.ShapeDtypeStruct((8 * steps, 256), f32),
        ],
        scratch_shapes=[
            pltpu.VMEM((2, 3 * ROWS, 256), bf),
            pltpu.VMEM((2, 3 * ROWS, 128), bf),
            pltpu.VMEM((128, 3 * ROWS), bf),
            pltpu.VMEM((128, 3 * ROWS), bf),
            pltpu.VMEM((3, WIN, 1024), f32),
            pltpu.VMEM((3, WIN, 1024), bf),
            pltpu.VMEM((3, WIN, 1024), bf),
            pltpu.VMEM((3, 1024, 128), bf),
            pltpu.VMEM((3, 1024, 128), bf),
            pltpu.VMEM((2, 3 * ROWS, 128), f32),
            pltpu.VMEM((2, 3 * ROWS, 128), f32),
        ],
        input_output_aliases=aliases,
        cost_estimate=pl.CostEstimate(
            flops=steps * 16 * 6 * 2 * 256 * WIN * ROWS,
            transcendentals=steps * 16 * WIN * ROWS,
            bytes_accessed=steps * 4 * 1024 * ROWS,
        ),
        compiler_params=pltpu.CompilerParams(vmem_limit_bytes=36 * 1024 * 1024),
    )(*args)


def on_device(query, key_proj, value, sinks, doc_ids, grad_out):
    queries, keys, values, grads = query[0], key_proj[0], value[0], grad_out[0]
    steps = PAIRS // CHUNKS
    own = []
    for c in range(CHUNKS):
        parts = []
        for i in range(c * steps, (c + 1) * steps):
            parts += [keys[:, i * 128 : (i + 1) * 128], values[:, i * 128 : (i + 1) * 128]]
        own.append(jnp.concatenate(parts, axis=1))
    near = [passed_along(x, "ctx", 1) for x in own]
    far = []
    far = [passed_along(x, "ctx", 1) for x in near]

    start = lax.axis_index("ctx") * ROWS
    front = SPAN * ROWS
    seg_pad = jnp.concatenate([jnp.full((front,), -1, jnp.int32), doc_ids[0]], axis=0)
    k_seg = lax.dynamic_slice_in_dim(seg_pad, start, front + ROWS)
    q_seg = k_seg[front:]
    feature = jnp.arange(128, dtype=jnp.int32)[None, :]
    f = ((feature <= q_seg[:, None]) & (feature < 64)).astype(jnp.bfloat16)
    t = jnp.where((feature > k_seg[:, None]) & (feature < 64), -FAR, 0.0).astype(jnp.bfloat16)
    sink_rows = jnp.repeat(sinks, TILE).reshape(H // 2, 2 * TILE)

    so_far, parts = None, []
    for c in range(CHUNKS):
        attended, grad_q, *rest = attend(
            c, queries, grads, (far[c], near[c], own[c]), f, t, sink_rows, so_far
        )
        so_far = (attended, grad_q)
        parts.append(rest)
        if c == 0:
            got = passed_along(rest[0], "ctx", -1)
    (_, near_0, own_0, sinks_0), (far_1, near_1, own_1, sinks_1) = parts

    def joined(share, came):
        return (share + came.astype(jnp.float32)).astype(jnp.bfloat16)

    half = 256 * steps
    got, far_1 = lax.optimization_barrier((got, far_1))
    both = jnp.concatenate([far_1, joined(near_0, got)], axis=1)
    both = passed_along(both, "ctx", -1)
    sink_grad = jnp.concatenate([jnp.sum(x.reshape(-1, TILE), axis=1) for x in (sinks_0, sinks_1)])
    devices = lax.axis_size("dp") * lax.axis_size("ctx")
    spread = jnp.broadcast_to(sink_grad[None], (devices, H))
    spread = lax.all_to_all(spread, ("dp", "ctx"), 0, 0, tiled=True)
    both, spread = lax.optimization_barrier((both, spread))
    last = passed_along(joined(near_1, both[:, :half]), "ctx", -1)
    sink_total = jnp.sum(spread, axis=0)
    grad_k, grad_v = [], []
    for total in (joined(own_0, both[:, half:]), joined(own_1, last)):
        for i in range(steps):
            grad_k.append(total[:, i * 256 : i * 256 + 128])
            grad_v.append(total[:, i * 256 + 128 : (i + 1) * 256])
    return (
        attended[None],
        grad_q[None],
        jnp.concatenate(grad_k, axis=1)[None],
        jnp.concatenate(grad_v, axis=1)[None],
        sink_total,
    )


def solution(mesh):
    in_specs = (
        P("dp", "ctx", None),
        P("dp", "ctx", None),
        P("dp", "ctx", None),
        P(),
        P("dp", None),
        P("dp", "ctx", None),
    )
    out_specs = (
        P("dp", "ctx", None),
        P("dp", "ctx", None),
        P("dp", "ctx", None),
        P("dp", "ctx", None),
        P(),
    )
    return jax.shard_map(
        on_device, mesh=mesh, in_specs=in_specs, out_specs=out_specs, check_vma=False
    )
```
